32 devices in a mesh: grp: 4 (over x, core), ex: 8 (over z, y).
Axes of the slice: x: 2, y: 2, z: 4, core: 2. Of those that a mesh axis runs over, the one named last changes fastest.
Arguments:
- item_ids: int32 [64, 256], P(('grp', 'ex')), may hold values from 0 to 32767, as said below
- lengths: int32 [64], P(('grp', 'ex')), may hold values from 32 to 256
- expert_ids: int32 [16384, 2], P(('grp', 'ex')), may hold values from 0 to 31, all different within a row; in each aligned block of 512 rows (0 to 511, 512 to 1023, ...) at most 48 rows name the same one
- gate_weights: float32 [16384, 2], P(('grp', 'ex')), may hold values from 0.1 to 1
- table: bfloat16 [32768, 512], P('ex'), may hold values from -6 to 6
- norm_gain: float32 [512], replicated, may hold values from 0.1 to 1.9
- w_gate: bfloat16 [32, 512, 1024], P('ex'), may hold values from -0.25 to 0.25
- w_up: bfloat16 [32, 512, 1024], P('ex'), may hold values from -0.25 to 0.25
- w_down: bfloat16 [32, 512, 1024], P('ex'), may hold values from -0.1875 to 0.1875
- d_out: bfloat16 [16384, 512], P(('grp', 'ex')), may hold values from -0.59765625 to 0.59765625
Outputs:
- layer_out: bfloat16 [16384, 512], P(('grp', 'ex'))
- grad_gate: float32 [32, 512, 1024], P('ex', None, 'grp')
- grad_up: float32 [32, 512, 1024], P('ex', None, 'grp')
- grad_down: float32 [32, 512, 1024], P('ex', None, 'grp')
The draws below stay inside these ranges and needn't reach their ends.
Inputs may be any that keep to these rules, and one draw needn't show every extreme that they name: `item_ids`: split the ids into blocks of 4096 consecutive values. Among the 512 positions of each aligned run of 2 sequences, at most 128 name ids of one such block, and in every such run some block is named exactly 128 times. `expert_ids`: each token names 2 different experts. Within each aligned block of 512 tokens no expert is named more than 48 times, and in some block some expert is named exactly 48 times.
All inputs are finite; a program needn't handle non-finite values.
Results may differ from the reference program's by a relative error of at most 0.012.
Values may be sent and summed in bfloat16 or wider, within the bound.
A program may use at most 128 MiB of HBM per device.

```python
import math
import jax
import jax.numpy as jnp
import numpy as np
from jax import lax

D = 512
FF = 1024
EXPERTS = 32
TOP = 2
SEQ = 256
ROWS_DEV = 4096
SEQS_DEV = 2
TOK_DEV = 512
ROW_CAP = 128
SEQUENCES = 64
TOKENS = 16384
VOCAB = 32768
CAP = 48
N_GRP = 4
N_EX = 8


def draw_item_ids(key, part):
    blocks = SEQUENCES // SEQS_DEV
    key_hot, key_perm, key_raw, key_span = jax.random.split(jax.random.fold_in(key, 4127), 4)
    hot = (jax.random.permutation(key_hot, blocks) % N_EX).astype(jnp.int32)
    within = jnp.arange(TOK_DEV, dtype=jnp.int32)

    def block_ids(hot_shard, perm_key, raw_key, span_key):
        others = (hot_shard + 1 + (within - ROW_CAP) % (N_EX - 1)) % N_EX
        shard = jnp.where(within < ROW_CAP, hot_shard, others)
        span = jax.random.randint(span_key, (TOK_DEV,), 1, ROWS_DEV + 1)
        raw = jax.random.randint(raw_key, (TOK_DEV,), 0, ROWS_DEV) % span
        row = (raw * 2897 + 1013) % ROWS_DEV
        row = jnp.where(within == 0, ROWS_DEV - 1, jnp.where(within == 1, 0, row))
        ids = (shard * ROWS_DEV + row).astype(jnp.int32)
        return ids[jax.random.permutation(perm_key, TOK_DEV)]
    result = jax.vmap(block_ids)(hot, jax.random.split(key_perm, blocks), jax.random.split(key_raw, blocks), jax.random.split(key_span, blocks))
    return result.reshape(SEQUENCES, SEQ).astype(jnp.int32)


def with_ends(values, rng, least, largest):
    index_at = [jax.random.randint(jax.random.fold_in(rng, axis), (), 0, length) for axis, length in enumerate(values.shape)]
    main_axis = values.shape.index(max(values.shape))
    next_to = index_at[:main_axis] + [(index_at[main_axis] + 1) % values.shape[main_axis]] + index_at[main_axis + 1:]
    return values.at[tuple(index_at)].set(least).at[tuple(next_to)].set(largest)


def levels(own_key, extent, pieces, least, largest):
    level = 1.0
    for dim, blocks in pieces:
        draws = jax.random.uniform(jax.random.fold_in(jax.random.fold_in(own_key, 6), dim), (blocks,), jnp.float32, least / len(pieces), largest / len(pieces))
        level = level * jnp.repeat(jnp.exp(draws), extent[dim] // blocks).reshape((-1,) + (1,) * (len(extent) - 1 - dim))
    return level


def routed_block(stream_key, own, number, rows, count, top, reach, skew):
    order = jax.random.permutation(stream_key, count)
    heavy_load, common = portions_of(count, rows * top, reach, skew, True), portions_of(count, rows * top, reach, skew, False)
    places = jnp.arange(count)

    def named(sizes, rotation):
        used = int((sizes > 0).sum())
        fixed = max(1, used // 4)
        passed = fixed + (places - fixed + rotation * (used - fixed)) % max(1, count - fixed)
        return jnp.zeros((count,), jnp.int32).at[order[jnp.where(places < fixed, places, passed)]].set(jnp.asarray(sizes, jnp.int32))

    sizes = jnp.where(number % 4 == 0, named(heavy_load, number // 4), named(common, number - number // 4 - 1))
    mixed = jax.random.permutation(jax.random.fold_in(own, 3), count)
    source_of, sink = mixed[0:count // 2 * 2:2], mixed[1:count // 2 * 2:2]
    slack = jnp.minimum(sizes[source_of] - 1, reach - sizes[sink]) // 2
    slack = jnp.where((source_of == order[0]) | (sink == order[0]) | (sizes[sink] == 0), 0, jnp.maximum(slack, 0))
    passed = jax.random.randint(jax.random.fold_in(own, 4), (count // 2,), 0, 1 << 20) % (slack + 1)
    sizes = sizes.at[source_of].add(-passed).at[sink].add(passed)
    labels = jnp.searchsorted(jnp.cumsum(sizes), jnp.arange(rows * top), side="right").astype(jnp.int32)
    listing = labels.reshape(top, rows).T
    listing = listing[jax.random.permutation(jax.random.fold_in(own, 1), rows)]
    rotation = jax.random.randint(jax.random.fold_in(own, 2), (rows, 1), 0, top)
    return jnp.take_along_axis(listing, (jnp.arange(top)[None, :] + rotation) % top, axis=1)


def portions_of(number_of, total, reach, skew, full):
    loads = [(1 << 20) // math.isqrt(standing ** skew) + 1 for standing in range(1, number_of + 1)]
    largest = reach if full else min(reach, max(-(-total // number_of), total * loads[0] // sum(loads)))
    least = 1 if total - largest >= number_of - 1 else 0
    holding, surplus = [largest] + [least] * (number_of - 1), total - largest - least * (number_of - 1)
    while surplus > 0:
        candidates = [i for i in range(1, number_of) if holding[i] < largest] or [i for i in range(1, number_of) if holding[i] < reach]
        pool, remaining = sum([loads[i] for i in candidates]), surplus
        for i in candidates:
            more = min(reach - holding[i], max(1, remaining * loads[i] // pool), surplus)
            holding[i] = holding[i] + more
            surplus = surplus - more
    return np.array(holding)


def noise(stream_key, shape, deviation, reach, cuts=(), kind=jnp.bfloat16):
    entries = jax.random.normal(stream_key, shape, jnp.float32) * deviation
    if len(cuts) > 0:
        entries = levels(stream_key, shape, cuts, -0.22, 0.18) * entries
    return jnp.clip(entries, min=-reach, max=reach).astype(kind)


def setup_inputs(seed: int = 0) -> dict:
    key_of = jax.random.split(jax.random.key(seed), 11)
    item_ids = draw_item_ids(jax.random.fold_in(key_of[10], 71), 0)
    lengths = with_ends(jax.random.randint(key_of[1], (SEQUENCES,), SEQ // 8, SEQ + 1), jax.random.fold_in(key_of[1], 1), SEQ // 8, SEQ).astype(jnp.int32)
    expert_ids_keys = jax.random.split(jax.random.fold_in(key_of[2], 1), TOKENS // TOK_DEV)
    expert_ids_turns = jax.random.permutation(jax.random.fold_in(key_of[2], 3), TOKENS // TOK_DEV)
    expert_ids = jax.vmap(lambda own, number: routed_block(jax.random.fold_in(key_of[2], 2), own, number, TOK_DEV, EXPERTS, TOP, CAP, 2))(expert_ids_keys, expert_ids_turns).reshape((TOKENS, TOP))
    gate_weights = jnp.clip(0.1 + 0.9 * jax.random.uniform(key_of[3], (TOKENS, TOP), jnp.float32) ** levels(key_of[3], (TOKENS, TOP), ((0, 32),), -0.2, 0.2), 0.1, 1.0)
    table = noise(key_of[4], (VOCAB, D), 1.0, 6.0, ((0, 8),))
    norm_gain = jnp.clip(1.0 + 0.18 * jax.random.normal(key_of[5], (D,), jnp.float32), 0.1, 1.9)
    w_gate = noise(key_of[6], (EXPERTS, D, FF), D ** -0.5, 0.25, ((0, 8),))
    w_up = noise(key_of[7], (EXPERTS, D, FF), D ** -0.5, 0.25, ((0, 8),))
    w_down = noise(key_of[8], (EXPERTS, D, FF), FF ** -0.5, 0.1875, ((0, 8),))
    d_out = noise(key_of[9], (TOKENS, D), 0.1, 0.59765625, ((0, 32),))
    return {"item_ids": item_ids, "lengths": lengths, "expert_ids": expert_ids, "gate_weights": gate_weights, "table": table, "norm_gain": norm_gain, "w_gate": w_gate, "w_up": w_up, "w_down": w_down, "d_out": d_out}


EPSILON = 1e-06

def reference(item_ids, lengths, expert_ids, gate_weights, table, norm_gain, w_gate, w_up, w_down, d_out):
    flat_ids = item_ids.reshape(-1).astype(jnp.int32)
    position = lax.broadcasted_iota(jnp.int32, item_ids.shape, 1)
    valid = (position < lengths[:, None]).reshape(-1)
    looked = jnp.take(table, flat_ids, axis=0).astype(jnp.float32)
    embedded = jnp.where(valid[:, None], looked, jnp.zeros_like(looked))
    mean_square = lax.optimization_barrier(jnp.mean(embedded * embedded, axis=1, keepdims=True))
    normed = (embedded * lax.rsqrt(mean_square + EPSILON) * norm_gain[None, :]).astype(jnp.bfloat16)
    cotangent = (gate_weights[:, :, None] * d_out[:, None, :].astype(jnp.float32)).astype(jnp.bfloat16)
    blocks = N_GRP * N_EX
    pair_expert = expert_ids.reshape(blocks, TOK_DEV * TOP).astype(jnp.int32)
    expert_iota = lax.broadcasted_iota(jnp.int32, (1, 1, EXPERTS), 2)
    onehot = (pair_expert[:, :, None] == expert_iota).astype(jnp.int32)
    rank = lax.optimization_barrier(jnp.sum((jnp.cumsum(onehot, axis=1) - onehot) * onehot, axis=2))
    source = lax.broadcasted_iota(jnp.int32, (blocks, 1), 0) % N_EX
    slots = (pair_expert * N_EX + source) * CAP + rank
    group_tokens = N_EX * TOK_DEV
    slots = slots.reshape(N_GRP, group_tokens, TOP)
    span = N_EX * CAP

    def one_expert(operands):
        rows_in, cot_in, gate_w, up_w, down_w = operands
        gate_pre = jnp.dot(rows_in, gate_w, preferred_element_type=jnp.float32)
        up_pre = jnp.dot(rows_in, up_w, preferred_element_type=jnp.float32)
        sigmoid = jax.nn.sigmoid(gate_pre)
        silu_gate = gate_pre * sigmoid
        active = (silu_gate * up_pre).astype(jnp.bfloat16)
        expert_out = jnp.dot(active, down_w.T, preferred_element_type=jnp.float32).astype(jnp.bfloat16)
        d_active = jnp.dot(cot_in, down_w, preferred_element_type=jnp.float32)
        d_gate = (d_active * up_pre * sigmoid * (1.0 + gate_pre * (1.0 - sigmoid))).astype(jnp.bfloat16)
        d_up = (d_active * silu_gate).astype(jnp.bfloat16)
        part_gate = jnp.dot(rows_in.T, d_gate, preferred_element_type=jnp.float32).astype(jnp.bfloat16)
        part_up = jnp.dot(rows_in.T, d_up, preferred_element_type=jnp.float32).astype(jnp.bfloat16)
        part_down = jnp.dot(cot_in.T, active, preferred_element_type=jnp.float32).astype(jnp.bfloat16)
        return (expert_out, part_gate, part_up, part_down)

    def one_group(carry, inputs):
        group_normed, group_cot, group_slots, group_embedded, group_gates = inputs
        empty = jnp.zeros((EXPERTS * span, D), jnp.bfloat16)
        buffer_rows = empty.at[group_slots].set(jnp.broadcast_to(group_normed[:, None, :], (group_tokens, TOP, D)))
        buffer_cot = empty.at[group_slots].set(group_cot)
        outs, part_gate, part_up, part_down = lax.map(one_expert, (buffer_rows.reshape(EXPERTS, span, D), buffer_cot.reshape(EXPERTS, span, D), w_gate, w_up, w_down))
        picked = jnp.take(outs.reshape(EXPERTS * span, D), group_slots, axis=0)
        mixed = group_embedded + lax.optimization_barrier(jnp.sum(group_gates[:, :, None] * picked.astype(jnp.float32), axis=1))
        parts = lax.optimization_barrier((part_gate, part_up, part_down))
        carry = (carry[0] + parts[0].astype(jnp.float32), carry[1] + parts[1].astype(jnp.float32), carry[2] + parts[2].astype(jnp.float32))
        return (carry, mixed.astype(jnp.bfloat16))
    zeros = jnp.zeros((EXPERTS, D, FF), jnp.float32)
    inputs = (normed.reshape(N_GRP, group_tokens, D), cotangent.reshape(N_GRP, group_tokens, TOP, D), slots, embedded.reshape(N_GRP, group_tokens, D), gate_weights.reshape(N_GRP, group_tokens, TOP))
    grads, mixed = lax.scan(one_group, (zeros, zeros, zeros), inputs)
    return (mixed.reshape(TOKENS, D), grads[0], grads[1], grads[2])
```

```python
import functools

import jax
import jax.numpy as jnp
from jax import lax
from jax.experimental import pallas as pl
from jax.experimental.pallas import tpu as pltpu
from jax.sharding import PartitionSpec as P

TOP = 2
CAP = 48
EPSILON = 1e-06
VMEM_BYTES = 56 * 1024 * 1024
MESH = pl.DeviceIdType.MESH
BF = jnp.bfloat16
F32 = jnp.float32


def iota(shape, dim):
    return lax.broadcasted_iota(jnp.int32, shape, dim)


def dot(a, b, dims=((1,), (0,))):
    return lax.dot_general(a, b, (dims, ((), ())), preferred_element_type=F32)


def fetch_kernel(
    n, groups, seqs, experts, row_cap,
    ids_row, ids_col, lens, e_row, g_row, table, gain, d_out,
    rows_in, cot_all, embedded,
    all_ids, key, local, packed, arrived, chosen, send_cot, send_rows,
    ids_s, ids_r, row_s, row_r, cot_s, cot_r, nrm_s, nrm_r, grp_s, grp_f, grp_r, own,
):
    me = lax.axis_index("ex")
    grp = lax.axis_index("grp")
    chips = groups // 2
    chip, core = grp // 2, grp % 2
    mate = chip * 2 + 1 - core
    rows_here, width = table.shape
    tok = ids_row.shape[1]
    block = experts // n * CAP

    barrier = pltpu.get_barrier_semaphore()
    for d in range(1, n):
        pl.semaphore_signal(barrier, inc=1, device_id={"ex": lax.rem(me + d, n)}, device_id_type=MESH)
    for d in range(1, chips):
        peer = lax.rem(chip + d, chips) * 2 + core
        pl.semaphore_signal(barrier, inc=1, device_id={"grp": peer}, device_id_type=MESH)
    pl.semaphore_signal(barrier, inc=1, device_id={"grp": mate}, device_id_type=MESH)
    pl.semaphore_wait(barrier, n - 1 + chips)

    def to_ex(src, dst, send, recv, d):
        peer = lax.rem(me + d, n)
        return pltpu.make_async_remote_copy(
            src_ref=src(peer), dst_ref=dst, send_sem=send.at[d], recv_sem=recv.at[d],
            device_id={"ex": peer}, device_id_type=MESH,
        )

    def ids_copy(d):
        return to_ex(lambda p: all_ids.at[me], all_ids.at[me], ids_s, ids_r, d)

    def row_copy(d):
        return to_ex(lambda p: packed.at[p], arrived.at[me], row_s, row_r, d)

    def cot_copy(d):
        return to_ex(lambda p: send_cot.at[p], cot_all.at[grp, me], cot_s, cot_r, d)

    def nrm_copy(d):
        return to_ex(lambda p: send_rows.at[p], rows_in.at[me], nrm_s, nrm_r, d)

    all_ids[me] = ids_row[...]
    for d in range(1, n):
        ids_copy(d).start()

    before = (iota((tok, tok), 0) < iota((tok, tok), 1)).astype(BF)
    e0, e1 = e_row[0:1, :], e_row[1:2, :]
    e_iota = iota((experts, tok), 0)
    hot0, hot1 = e_iota == e0, e_iota == e1
    hot = jnp.where(hot0, 1.0, jnp.where(hot1, 1.0, 0.0)).astype(BF)
    earlier = dot(hot, before)
    slot0 = e0 * CAP + jnp.sum(jnp.where(hot0, earlier, 0.0), axis=0, keepdims=True).astype(jnp.int32)
    slot1 = e1 * CAP + jnp.sum(jnp.where(hot1, earlier, 0.0), axis=0, keepdims=True).astype(jnp.int32)
    g0, g1 = g_row[0:1, :], g_row[1:2, :]
    for p in range(n):
        s_iota = iota((block, tok), 0) + p * block
        m0, m1 = s_iota == slot0, s_iota == slot1
        weight = jnp.sum(jnp.where(m0, g0, jnp.where(m1, g1, 0.0)), axis=1, keepdims=True)
        chosen[p] = jnp.where(m0, 1.0, jnp.where(m1, 1.0, 0.0)).astype(BF)
        send_cot[p] = (weight * dot(chosen[p], d_out[...])).astype(BF)
    for d in range(1, n):
        cot_copy(d).start()
    own_cot = pltpu.make_async_copy(send_cot.at[me], cot_all.at[grp, me], own.at[0])
    own_cot.start()

    for d in range(1, n):
        ids_copy(d).wait_recv()
    ids = jnp.concatenate([all_ids[r] for r in range(n)], axis=0)
    here = ids - me * rows_here
    mine = (here >= 0) & (here < rows_here)
    order = dot(jnp.where(mine, 1.0, 0.0).astype(BF), before)
    keys = jnp.where(mine, order.astype(jnp.int32), -1)
    for r in range(n):
        key[r] = keys[r : r + 1, :]
        local[r] = jnp.where(mine, here, 0)[r : r + 1, :].astype(F32)

    def pick(r):
        hit = iota((row_cap, tok), 0) == key[r]
        return jnp.sum(jnp.where(hit, local[r], 0.0), axis=1, keepdims=True).astype(jnp.int32)

    @pl.loop(0, n // 2)
    def _(i):
        first = lax.rem(me + 1 + 2 * i, n)
        second = lax.rem(me + 2 + 2 * i, n)
        index = jnp.concatenate([pick(first), pick(second)], axis=0)
        onehot = jnp.where(iota((2 * row_cap, rows_here), 1) == index, 1.0, 0.0).astype(BF)
        got = dot(onehot, table[...]).astype(BF)
        packed[first] = got[:row_cap]
        packed[second] = got[row_cap:]
        row_copy(2 * i + 1).start()

        @pl.when(i < n // 2 - 1)
        def _():
            row_copy(2 * i + 2).start()

    arrived[me] = packed[me]

    ids_c = ids_col[...]
    h_iota = iota((tok, n), 1)
    base = h_iota * rows_here
    hot_h = jnp.where((ids_c >= base) & (ids_c < base + rows_here), 1.0, 0.0)
    after = (iota((tok, tok), 0) > iota((tok, tok), 1)).astype(BF)
    ahead = dot(after, hot_h.astype(BF)) + (h_iota * row_cap).astype(F32)
    place = jnp.sum(ahead * hot_h, axis=1, keepdims=True).astype(jnp.int32)
    find = jnp.where(iota((tok, n * row_cap), 1) == place, 1.0, 0.0).astype(BF)
    t_iota = iota((tok, 1), 0)
    length = tok // seqs
    valid = jnp.zeros((tok, 1), F32)
    for s in range(seqs):
        inside = (t_iota >= s * length) & (t_iota < s * length + lens[s])
        valid = jnp.where(inside, 1.0, valid)
    for d in range(1, n):
        row_copy(d).wait_recv()
    emb = dot(find, arrived[...].reshape(n * row_cap, width))
    emb = jnp.where(valid > 0.5, emb, 0.0)
    embedded[...] = emb.astype(BF)
    mean_square = jnp.mean(emb * emb, axis=1, keepdims=True)
    normed = (emb * lax.rsqrt(mean_square + EPSILON) * gain[...]).astype(BF)
    for p in range(n):
        send_rows[p] = dot(chosen[p], normed).astype(BF)
    for d in range(1, n):
        nrm_copy(d).start()
    own_rows = pltpu.make_async_copy(send_rows.at[me], rows_in.at[me], own.at[1])
    own_rows.start()

    def to_grp(b, peer, send, recv):
        return pltpu.make_async_remote_copy(
            src_ref=cot_all.at[b], dst_ref=cot_all.at[b], send_sem=send, recv_sem=recv,
            device_id={"grp": peer}, device_id_type=MESH,
        )

    def across(d):
        peer = lax.rem(chip + d, chips) * 2 + core
        return to_grp(grp, peer, grp_s.at[d], grp_r.at[d])

    def to_mate(d):
        source = lax.rem(chip - d + chips, chips) * 2 + core
        return to_grp(source, mate, grp_f.at[d], grp_r.at[chips + d])

    for d in range(1, n):
        cot_copy(d).wait_recv()
    own_cot.wait()
    for d in range(1, chips):
        across(d).start()
    to_mate(0).start()
    for d in range(1, chips):
        across(d).wait_recv()
        to_mate(d).start()
    for d in range(chips):
        to_mate(d).wait_recv()
        to_mate(d).wait_send()
    for d in range(1, chips):
        across(d).wait_send()
    for d in range(1, n):
        nrm_copy(d).wait_recv()
        for copy in (ids_copy, row_copy, cot_copy, nrm_copy):
            copy(d).wait_send()
    own_rows.wait()


def sigmoid_of(v):
    return 1.0 / (1.0 + jnp.exp(-v))


def forward_kernel(rows, w_gate, w_up, w_down, out):
    n, _, cap, width = rows.shape
    x = rows[...].reshape(n * cap, width)
    gate = dot(x, w_gate[0])
    up = dot(x, w_up[0])
    active = (gate * sigmoid_of(gate) * up).astype(BF)
    out[...] = dot(active, w_down[0], ((1,), (1,))).astype(BF).reshape(n, 1, cap, width)


def grad_kernel(_, rows, cot, w_gate, w_up, w_down, o_gate, o_up, o_down):
    g, n, _, cap, width = rows.shape
    x = rows[...].reshape(g * n * cap, width)
    c = cot[...].reshape(g * n * cap, width)
    gate = dot(x, w_gate[0])
    up = dot(x, w_up[0])
    d_active = dot(c, w_down[0])
    sigmoid = sigmoid_of(gate)
    silu = gate * sigmoid
    active = (silu * up).astype(BF)
    d_gate = (d_active * up * sigmoid * (1.0 + gate * (1.0 - sigmoid))).astype(BF)
    d_up = (d_active * silu).astype(BF)
    o_down[0] = dot(c, active, ((0,), (0,)))
    o_gate[0] = dot(x, d_gate, ((0,), (0,)))
    o_up[0] = dot(x, d_up, ((0,), (0,)))


def mix_kernel(experts, expert_ids, gates, embedded, returned, out):
    tok = embedded.shape[0]
    ids = expert_ids[...]
    e_iota = iota((tok, experts), 1)
    hots = [e_iota == ids[:, k : k + 1] for k in range(TOP)]
    hot = jnp.where(hots[0], 1.0, jnp.where(hots[1], 1.0, 0.0)).astype(BF)
    after = (iota((tok, tok), 0) > iota((tok, tok), 1)).astype(BF)
    earlier = dot(after, hot)
    total = embedded[...].astype(F32)
    mixed = jnp.zeros_like(total)
    for k in range(TOP):
        rank = jnp.sum(jnp.where(hots[k], earlier, 0.0), axis=1, keepdims=True).astype(jnp.int32)
        slot = ids[:, k : k + 1] * CAP + rank
        pick = jnp.where(iota((tok, experts * CAP), 1) == slot, 1.0, 0.0).astype(BF)
        mixed = mixed + gates[:, k : k + 1] * dot(pick, returned[...])
    out[...] = (total + mixed).astype(BF)


def on_device(
    item_ids, lengths, expert_ids, gate_weights, table, norm_gain, w_gate, w_up, w_down, d_out
):
    n = lax.axis_size("ex")
    groups = lax.axis_size("grp")
    seqs, length = item_ids.shape
    tok = seqs * length
    width = table.shape[1]
    exp_here = w_gate.shape[0]
    hidden = w_gate.shape[2]
    part = hidden // groups
    experts = exp_here * n
    row_cap = tok // 4
    block = exp_here * CAP
    vmem = pl.BlockSpec(memory_space=pltpu.VMEM)
    dma = pltpu.SemaphoreType.DMA
    rows_in, cot_all, embedded = pl.pallas_call(
        functools.partial(fetch_kernel, n, groups, seqs, experts, row_cap),
        out_shape=(
            jax.ShapeDtypeStruct((n, block, width), BF),
            jax.ShapeDtypeStruct((groups, n, block, width), BF),
            jax.ShapeDtypeStruct((tok, width), BF),
        ),
        in_specs=[vmem, vmem, pl.BlockSpec(memory_space=pltpu.SMEM)] + [vmem] * 5,
        out_specs=(pl.BlockSpec(memory_space=pl.ANY), pl.BlockSpec(memory_space=pl.ANY), vmem),
        scratch_shapes=[
            pltpu.VMEM((n, 1, tok), jnp.int32),
            pltpu.VMEM((n, 1, tok), jnp.int32),
            pltpu.VMEM((n, 1, tok), F32),
            pltpu.VMEM((n, row_cap, width), BF),
            pltpu.VMEM((n, row_cap, width), BF),
            pltpu.VMEM((n, block, tok), BF),
            pltpu.VMEM((n, block, width), BF),
            pltpu.VMEM((n, block, width), BF),
        ]
        + [dma((n,))] * 8
        + [dma((groups,)), dma((groups,)), dma((groups,)), dma((2,))],
        compiler_params=pltpu.CompilerParams(
            collective_id=0, has_side_effects=True, vmem_limit_bytes=VMEM_BYTES
        ),
    )(
        item_ids.reshape(1, tok),
        item_ids.reshape(tok, 1),
        lengths,
        expert_ids.T,
        gate_weights.T,
        table,
        norm_gain.reshape(1, width),
        d_out,
    )
    rows_all = lax.all_gather(rows_in, "grp", axis=0)
    local_params = pltpu.CompilerParams(vmem_limit_bytes=VMEM_BYTES)
    flops = 2 * n * block * width * hidden
    whole = lambda: pl.BlockSpec((1, width, hidden), lambda j: (j, 0, 0))
    expert_out = pl.pallas_call(
        forward_kernel,
        grid=(exp_here,),
        in_specs=[pl.BlockSpec((n, 1, CAP, width), lambda j: (0, j, 0, 0)), whole(), whole(), whole()],
        out_specs=pl.BlockSpec((n, 1, CAP, width), lambda j: (0, j, 0, 0)),
        out_shape=jax.ShapeDtypeStruct((n, exp_here, CAP, width), BF),
        compiler_params=local_params,
        cost_estimate=pl.CostEstimate(flops=3 * flops, bytes_accessed=2**24, transcendentals=0),
    )(rows_in.reshape(n, exp_here, CAP, width), w_gate, w_up, w_down)
    returned = lax.all_to_all(
        expert_out.reshape(n, block, width), "ex", split_axis=0, concat_axis=0, tiled=True
    )
    shape = (groups, n, exp_here, CAP, width)
    rows_spec = lambda: pl.BlockSpec((groups, n, 1, CAP, width), lambda j, q: (0, 0, j, 0, 0))
    weight_spec = lambda: pl.BlockSpec((1, width, part), lambda j, q: (j, 0, q[0]))
    grads = pl.pallas_call(
        grad_kernel,
        grid_spec=pltpu.PrefetchScalarGridSpec(
            num_scalar_prefetch=1,
            grid=(exp_here,),
            in_specs=[rows_spec(), rows_spec(), weight_spec(), weight_spec(), weight_spec()],
            out_specs=[pl.BlockSpec((1, width, part), lambda j, q: (j, 0, 0))] * 3,
        ),
        out_shape=[jax.ShapeDtypeStruct((exp_here, width, part), F32)] * 3,
        compiler_params=local_params,
        cost_estimate=pl.CostEstimate(flops=6 * flops, bytes_accessed=2**24, transcendentals=0),
    )(
        lax.axis_index("grp").reshape(1).astype(jnp.int32),
        rows_all.reshape(shape),
        cot_all.reshape(shape),
        w_gate,
        w_up,
        w_down,
    )
    output = pl.pallas_call(
        functools.partial(mix_kernel, experts),
        in_specs=[vmem] * 4,
        out_specs=vmem,
        out_shape=jax.ShapeDtypeStruct((tok, width), BF),
        compiler_params=local_params,
        cost_estimate=pl.CostEstimate(flops=flops, bytes_accessed=2**22, transcendentals=0),
    )(expert_ids, gate_weights, embedded, returned.reshape(experts * CAP, width))
    return (output, grads[0], grads[1], grads[2])


def solution(mesh):
    placed = (
        P(("grp", "ex"), None),
        P(("grp", "ex")),
        P(("grp", "ex"), None),
        P(("grp", "ex"), None),
        P("ex", None),
        P(),
        P("ex", None, None),
        P("ex", None, None),
        P("ex", None, None),
        P(("grp", "ex"), None),
    )
    return jax.shard_map(
        on_device,
        mesh=mesh,
        in_specs=placed,
        out_specs=(
            P(("grp", "ex"), None),
            P("ex", None, "grp"),
            P("ex", None, "grp"),
            P("ex", None, "grp"),
        ),
        check_vma=False,
    )
```

```python
import functools

import jax
import jax.numpy as jnp
from jax import lax
from jax.experimental import pallas as pl
from jax.experimental.pallas import tpu as pltpu
from jax.sharding import PartitionSpec as P

TOP = 2
CAP = 48
EPSILON = 1e-06
VMEM_BYTES = 60 * 1024 * 1024
MESH = pl.DeviceIdType.MESH
BF = jnp.bfloat16
F32 = jnp.float32


def iota(shape, dim):
    return lax.broadcasted_iota(jnp.int32, shape, dim)


def dot(a, b, dims=((1,), (0,))):
    return lax.dot_general(a, b, (dims, ((), ())), preferred_element_type=F32)


def sigmoid_of(v):
    return 1.0 / (1.0 + jnp.exp(-v))


def layer_kernel(
    n, groups, seqs, experts, row_cap,
    ids_row, ids_col, lens, e_row, g_row, e_col, g_col, gain, d_out, table_h, gate_h, up_h, down_h,
    out, o_gate, o_up, o_down,
    all_ids, key, local, packed, arrived, chosen, send_cot, send_rows, rows_all, cot_all,
    expert_out, returned, table, w_gate, w_up, w_down, stage,
    ids_s, ids_r, row_s, row_r, cot_s, cot_r, nrm_s, nrm_r, ret_s, ret_r,
    cx_s, cx_r, cm_s, cm_r, rx_s, rx_r, rm_s, rm_r, load_s, stage_s,
):
    me = lax.axis_index("ex")
    grp = lax.axis_index("grp")
    chips = groups // 2
    chip, core = grp // 2, grp % 2
    mate = chip * 2 + 1 - core
    rows_here, width = table.shape
    tok = ids_row.shape[1]
    exp_here = experts // n
    block = exp_here * CAP
    part = o_gate.shape[2]
    loads = [
        pltpu.make_async_copy(src, dst, load_s.at[i])
        for i, (src, dst) in enumerate(
            [(table_h, table), (gate_h, w_gate), (up_h, w_up), (down_h, w_down)]
        )
    ]
    for load in loads:
        load.start()

    barrier = pltpu.get_barrier_semaphore()
    for d in range(1, n):
        pl.semaphore_signal(barrier, inc=1, device_id={"ex": lax.rem(me + d, n)}, device_id_type=MESH)
    for d in range(1, chips):
        peer = lax.rem(chip + d, chips) * 2 + core
        pl.semaphore_signal(barrier, inc=1, device_id={"grp": peer}, device_id_type=MESH)
    pl.semaphore_signal(barrier, inc=1, device_id={"grp": mate}, device_id_type=MESH)
    pl.semaphore_wait(barrier, n - 1 + chips)

    def to_ex(src, dst, send, recv, d):
        peer = lax.rem(me + d, n)
        return pltpu.make_async_remote_copy(
            src_ref=src(peer), dst_ref=dst, send_sem=send.at[d], recv_sem=recv.at[d],
            device_id={"ex": peer}, device_id_type=MESH,
        )

    def ids_copy(d):
        return to_ex(lambda p: all_ids.at[me], all_ids.at[me], ids_s, ids_r, d)

    def row_copy(d):
        return to_ex(lambda p: packed.at[p], arrived.at[me], row_s, row_r, d)

    def cot_copy(d):
        return to_ex(lambda p: send_cot.at[p], cot_all.at[grp, me], cot_s, cot_r, d)

    def nrm_copy(d, j):
        return to_ex(
            lambda p: send_rows.at[p, j], rows_all.at[grp, j, me], nrm_s.at[j], nrm_r.at[j], d
        )

    def ret_copy(d, j):
        return to_ex(lambda p: expert_out.at[j, p], returned.at[me, j], ret_s.at[j], ret_r.at[j], d)

    def across(held, send, recv, d):
        peer = lax.rem(chip + d, chips) * 2 + core
        return pltpu.make_async_remote_copy(
            src_ref=held(grp), dst_ref=held(grp), send_sem=send.at[d], recv_sem=recv.at[d],
            device_id={"grp": peer}, device_id_type=MESH,
        )

    def to_mate(held, send, recv, d):
        source = lax.rem(chip - d + chips, chips) * 2 + core
        return pltpu.make_async_remote_copy(
            src_ref=held(source), dst_ref=held(source), send_sem=send.at[d], recv_sem=recv.at[d],
            device_id={"grp": mate}, device_id_type=MESH,
        )

    def cot_across(d):
        return across(lambda b: cot_all.at[b], cx_s, cx_r, d)

    def cot_mate(d):
        return to_mate(lambda b: cot_all.at[b], cm_s, cm_r, d)

    def rows_across(d, j):
        return across(lambda b: rows_all.at[b, j], rx_s.at[j], rx_r.at[j], d)

    def rows_mate(d, j):
        return to_mate(lambda b: rows_all.at[b, j], rm_s.at[j], rm_r.at[j], d)

    all_ids[me] = ids_row[...]
    for d in range(1, n):
        ids_copy(d).start()

    before = (iota((tok, tok), 0) < iota((tok, tok), 1)).astype(BF)
    e0, e1 = e_row[0:1, :], e_row[1:2, :]
    e_iota = iota((experts, tok), 0)
    hot0, hot1 = e_iota == e0, e_iota == e1
    hot = jnp.where(hot0, 1.0, jnp.where(hot1, 1.0, 0.0)).astype(BF)
    earlier = dot(hot, before)
    slot0 = e0 * CAP + jnp.sum(jnp.where(hot0, earlier, 0.0), axis=0, keepdims=True).astype(jnp.int32)
    slot1 = e1 * CAP + jnp.sum(jnp.where(hot1, earlier, 0.0), axis=0, keepdims=True).astype(jnp.int32)
    g0, g1 = g_row[0:1, :], g_row[1:2, :]
    for p in range(n):
        s_iota = iota((block, tok), 0) + p * block
        m0, m1 = s_iota == slot0, s_iota == slot1
        weight = jnp.sum(jnp.where(m0, g0, jnp.where(m1, g1, 0.0)), axis=1, keepdims=True)
        chosen[p] = jnp.where(m0, 1.0, jnp.where(m1, 1.0, 0.0)).astype(BF)
        mine_cot = weight * dot(chosen[p], d_out[...])
        send_cot[p] = mine_cot.astype(BF).reshape(exp_here, CAP, width)
    for d in range(1, n):
        cot_copy(d).start()
    cot_all[grp, me] = send_cot[me]

    for d in range(1, n):
        ids_copy(d).wait_recv()
    ids = jnp.concatenate([all_ids[r] for r in range(n)], axis=0)
    here = ids - me * rows_here
    mine = (here >= 0) & (here < rows_here)
    order = dot(jnp.where(mine, 1.0, 0.0).astype(BF), before)
    keys = jnp.where(mine, order.astype(jnp.int32), -1)
    for r in range(n):
        key[r] = keys[r : r + 1, :]
        local[r] = jnp.where(mine, here, 0)[r : r + 1, :].astype(F32)

    def pick(r):
        hit = iota((row_cap, tok), 0) == key[r]
        return jnp.sum(jnp.where(hit, local[r], 0.0), axis=1, keepdims=True).astype(jnp.int32)

    loads[0].wait()

    @pl.loop(0, n // 2)
    def _(i):
        first = lax.rem(me + 1 + 2 * i, n)
        second = lax.rem(me + 2 + 2 * i, n)
        index = jnp.concatenate([pick(first), pick(second)], axis=0)
        onehot = jnp.where(iota((2 * row_cap, rows_here), 1) == index, 1.0, 0.0).astype(BF)
        got = dot(onehot, table[...]).astype(BF)
        packed[first] = got[:row_cap]
        packed[second] = got[row_cap:]
        row_copy(2 * i + 1).start()

        @pl.when(i < n // 2 - 1)
        def _():
            row_copy(2 * i + 2).start()

    arrived[me] = packed[me]

    ids_c = ids_col[...]
    h_iota = iota((tok, n), 1)
    base = h_iota * rows_here
    hot_h = jnp.where((ids_c >= base) & (ids_c < base + rows_here), 1.0, 0.0)
    after = (iota((tok, tok), 0) > iota((tok, tok), 1)).astype(BF)
    ahead = dot(after, hot_h.astype(BF)) + (h_iota * row_cap).astype(F32)
    place = jnp.sum(ahead * hot_h, axis=1, keepdims=True).astype(jnp.int32)
    find = jnp.where(iota((tok, n * row_cap), 1) == place, 1.0, 0.0).astype(BF)
    t_iota = iota((tok, 1), 0)
    length = tok // seqs
    valid = jnp.zeros((tok, 1), F32)
    for s in range(seqs):
        inside = (t_iota >= s * length) & (t_iota < s * length + lens[s])
        valid = jnp.where(inside, 1.0, valid)
    col = e_col[...]
    c_iota = iota((tok, experts), 1)
    hots = [c_iota == col[:, k : k + 1] for k in range(TOP)]
    spans = experts * CAP // width
    hot_c = jnp.where(hots[0], 1.0, jnp.where(hots[1], 1.0, 0.0)).astype(BF)
    earlier_c = dot(after, hot_c)
    for k in range(TOP):
        rank = jnp.sum(jnp.where(hots[k], earlier_c, 0.0), axis=1, keepdims=True)
        slot = col[:, k : k + 1] * CAP + rank.astype(jnp.int32)
        for i in range(spans):
            hit = iota((tok, width), 1) + i * width == slot
            table[pl.ds((k * spans + i) * tok, tok)] = jnp.where(hit, 1.0, 0.0).astype(BF)

    for d in range(1, n):
        cot_copy(d).wait_recv()
    for d in range(1, chips):
        cot_across(d).start()
    cot_mate(0).start()

    for d in range(1, n):
        row_copy(d).wait_recv()
    emb = dot(find, arrived[...].reshape(n * row_cap, width))
    emb = jnp.where(valid > 0.5, emb, 0.0)
    out[...] = emb.astype(BF)
    mean_square = jnp.mean(emb * emb, axis=1, keepdims=True)
    normed = (emb * lax.rsqrt(mean_square + EPSILON) * gain[...]).astype(BF)
    for p in range(n):
        send_rows[p] = dot(chosen[p], normed).astype(BF).reshape(exp_here, CAP, width)

    @pl.loop(0, exp_here)
    def _(j):
        for d in range(1, n):
            nrm_copy(d, j).start()
        rows_all[grp, j, me] = send_rows[me, j]

    for d in range(1, chips):
        cot_across(d).wait_recv()
        cot_mate(d).start()
    for load in loads[1:]:
        load.wait()

    @pl.loop(0, exp_here)
    def _(j):
        for d in range(1, n):
            nrm_copy(d, j).wait_recv()
        for d in range(1, chips):
            rows_across(d, j).start()
        rows_mate(0, j).start()
        x = rows_all[grp, j].reshape(n * CAP, width)
        gate = dot(x, w_gate[j])
        up = dot(x, w_up[j])
        active = (gate * sigmoid_of(gate) * up).astype(BF)
        result = dot(active, w_down[j], ((1,), (1,))).astype(BF)
        expert_out[j] = result.reshape(n, CAP, width)
        for d in range(1, n):
            ret_copy(d, j).start()
        returned[me, j] = expert_out[j, me]

    for d in range(chips):
        cot_mate(d).wait_recv()

    def pass_on(j):
        for d in range(1, chips):
            rows_across(d, j).wait_recv()
            rows_mate(d, j).start()

    def write(j, k):
        target = (o_gate, o_up, o_down)[k]
        return pltpu.make_async_copy(stage.at[j % 2, k], target.at[j], stage_s.at[j % 2, k])

    pass_on(0)
    columns = pl.ds(pl.multiple_of(grp * part, part), part)

    @pl.loop(0, exp_here)
    def _(j):
        @pl.when(j < exp_here - 1)
        def _():
            pass_on(j + 1)

        for d in range(chips):
            rows_mate(d, j).wait_recv()

        @pl.when(j >= 2)
        def _():
            for k in range(3):
                write(j - 2, k).wait()

        few = max(1, min(groups, 256 // (n * n)))
        for b in range(0, groups, few):
            some = pl.ds(b, min(few, groups - b))
            x = rows_all[some, j].reshape(-1, width)
            c = cot_all[some, :, j].reshape(-1, width)
            gate = dot(x, w_gate[j, :, columns])
            up = dot(x, w_up[j, :, columns])
            d_active = dot(c, w_down[j, :, columns])
            sigmoid = sigmoid_of(gate)
            silu = gate * sigmoid
            active = (silu * up).astype(BF)
            d_gate = (d_active * up * sigmoid * (1.0 + gate * (1.0 - sigmoid))).astype(BF)
            d_up = (d_active * silu).astype(BF)
            for k, (left, right) in enumerate([(x, d_gate), (x, d_up), (c, active)]):
                term = dot(left, right, ((0,), (0,)))
                stage[j % 2, k] = term if b == 0 else stage[j % 2, k] + term
        for k in range(3):
            write(j, k).start()

    @pl.loop(0, exp_here)
    def _(j):
        for d in range(1, n):
            ret_copy(d, j).wait_recv()

    back = returned[...].reshape(experts * CAP, width)
    mixed = jnp.zeros((tok, width), F32)
    for k in range(TOP):
        picked = jnp.zeros((tok, width), F32)
        for i in range(spans):
            pick_part = table[pl.ds((k * spans + i) * tok, tok)]
            picked = picked + dot(pick_part, back[i * width : (i + 1) * width])
        mixed = mixed + g_col[:, k : k + 1] * picked
    out[...] = (out[...].astype(F32) + mixed).astype(BF)

    for j in range(max(0, exp_here - 2), exp_here):
        for k in range(3):
            write(j, k).wait()
    for d in range(1, n):
        for copy in (ids_copy, row_copy, cot_copy):
            copy(d).wait_send()
    for d in range(1, chips):
        cot_across(d).wait_send()
    for d in range(chips):
        cot_mate(d).wait_send()

    @pl.loop(0, exp_here)
    def _(j):
        for d in range(1, n):
            nrm_copy(d, j).wait_send()
            ret_copy(d, j).wait_send()
        for d in range(1, chips):
            rows_across(d, j).wait_send()
        for d in range(chips):
            rows_mate(d, j).wait_send()


def on_device(
    item_ids, lengths, expert_ids, gate_weights, table, norm_gain, w_gate, w_up, w_down, d_out
):
    n = lax.axis_size("ex")
    groups = lax.axis_size("grp")
    seqs, length = item_ids.shape
    tok = seqs * length
    width = table.shape[1]
    exp_here, _, hidden = w_gate.shape
    part = hidden // groups
    experts = exp_here * n
    row_cap = tok // 4
    block = exp_here * CAP
    chips = groups // 2
    vmem = pl.BlockSpec(memory_space=pltpu.VMEM)
    hbm = pl.BlockSpec(memory_space=pl.ANY)
    dma = pltpu.SemaphoreType.DMA
    grad = jax.ShapeDtypeStruct((exp_here, width, part), F32)
    return pl.pallas_call(
        functools.partial(layer_kernel, n, groups, seqs, experts, row_cap),
        out_shape=(jax.ShapeDtypeStruct((tok, width), BF), grad, grad, grad),
        in_specs=[vmem, vmem, pl.BlockSpec(memory_space=pltpu.SMEM)] + [vmem] * 6 + [hbm] * 4,
        out_specs=(vmem, hbm, hbm, hbm),
        scratch_shapes=[
            pltpu.VMEM((n, 1, tok), jnp.int32),
            pltpu.VMEM((n, 1, tok), jnp.int32),
            pltpu.VMEM((n, 1, tok), F32),
            pltpu.VMEM((n, row_cap, width), BF),
            pltpu.VMEM((n, row_cap, width), BF),
            pltpu.VMEM((n, block, tok), BF),
            pltpu.VMEM((n, exp_here, CAP, width), BF),
            pltpu.VMEM((n, exp_here, CAP, width), BF),
            pltpu.VMEM((groups, exp_here, n, CAP, width), BF),
            pltpu.VMEM((groups, n, exp_here, CAP, width), BF),
            pltpu.VMEM((exp_here, n, CAP, width), BF),
            pltpu.VMEM((n, exp_here, CAP, width), BF),
            pltpu.VMEM(table.shape, BF),
            pltpu.VMEM(w_gate.shape, BF),
            pltpu.VMEM(w_up.shape, BF),
            pltpu.VMEM(w_down.shape, BF),
            pltpu.VMEM((2, 3, width, part), F32),
        ]
        + [dma((n,))] * 6
        + [dma((exp_here, n))] * 4
        + [dma((chips,))] * 4
        + [dma((exp_here, chips))] * 4
        + [dma((4,)), dma((2, 3))],
        compiler_params=pltpu.CompilerParams(
            collective_id=0, has_side_effects=True, vmem_limit_bytes=VMEM_BYTES
        ),
    )(
        item_ids.reshape(1, tok),
        item_ids.reshape(tok, 1),
        lengths,
        expert_ids.T,
        gate_weights.T,
        expert_ids,
        gate_weights,
        norm_gain.reshape(1, width),
        d_out,
        table,
        w_gate,
        w_up,
        w_down,
    )


def solution(mesh):
    placed = (
        P(("grp", "ex"), None),
        P(("grp", "ex")),
        P(("grp", "ex"), None),
        P(("grp", "ex"), None),
        P("ex", None),
        P(),
        P("ex", None, None),
        P("ex", None, None),
        P("ex", None, None),
        P(("grp", "ex"), None),
    )
    return jax.shard_map(
        on_device,
        mesh=mesh,
        in_specs=placed,
        out_specs=(
            P(("grp", "ex"), None),
            P("ex", None, "grp"),
            P("ex", None, "grp"),
            P("ex", None, "grp"),
        ),
        check_vma=False,
    )
```

```python
import functools

import jax
import jax.numpy as jnp
from jax import lax
from jax.experimental import pallas as pl
from jax.experimental.pallas import tpu as pltpu
from jax.sharding import PartitionSpec as P

TOP = 2
CAP = 48
EPSILON = 1e-06
VMEM_BYTES = 60 * 1024 * 1024
MESH = pl.DeviceIdType.MESH
BF = jnp.bfloat16
F32 = jnp.float32


def iota(shape, dim):
    return lax.broadcasted_iota(jnp.int32, shape, dim)


def dot(a, b, dims=((1,), (0,))):
    return lax.dot_general(a, b, (dims, ((), ())), preferred_element_type=F32)


def sigmoid_of(v):
    return 1.0 / (1.0 + jnp.exp(-v))


def layer_kernel(
    n, groups, seqs, experts, row_cap,
    ids_here, lens, e_row, g_row, gain, d_out, table_h, gate_h, up_h, down_h,
    out, o_gate, o_up, o_down,
    all_ids, key, local, packed, arrived, chosen, send_cot, send_rows, rows_all, cot_all,
    expert_out, returned, table, w_gate, w_up, w_down, stage,
    ids_s, ids_r, row_s, row_r, cot_s, cot_r, nrm_s, nrm_r, ret_s, ret_r,
    cx_s, cx_r, cm_s, cm_r, rx_s, rx_r, rm_s, rm_r, load_s, stage_s,
):
    me = lax.axis_index("ex")
    grp = lax.axis_index("grp")
    chips = groups // 2
    chip, core = grp // 2, grp % 2
    mate = chip * 2 + 1 - core
    rows_here, width = table.shape
    tok = e_row.shape[1]
    exp_here = experts // n
    block = exp_here * CAP
    part = o_gate.shape[2]
    loads = [
        pltpu.make_async_copy(src, dst, load_s.at[i])
        for i, (src, dst) in enumerate(
            [(table_h, table), (gate_h, w_gate), (up_h, w_up), (down_h, w_down)]
        )
    ]
    for load in loads:
        load.start()

    barrier = pltpu.get_barrier_semaphore()
    for d in range(1, n):
        pl.semaphore_signal(barrier, inc=1, device_id={"ex": lax.rem(me + d, n)}, device_id_type=MESH)
    for d in range(1, chips):
        peer = lax.rem(chip + d, chips) * 2 + core
        pl.semaphore_signal(barrier, inc=1, device_id={"grp": peer}, device_id_type=MESH)
    pl.semaphore_signal(barrier, inc=1, device_id={"grp": mate}, device_id_type=MESH)
    pl.semaphore_wait(barrier, n - 1 + chips)

    def to_ex(src, dst, send, recv, d):
        peer = lax.rem(me + d, n)
        return pltpu.make_async_remote_copy(
            src_ref=src(peer), dst_ref=dst, send_sem=send.at[d], recv_sem=recv.at[d],
            device_id={"ex": peer}, device_id_type=MESH,
        )

    def ids_copy(d):
        return to_ex(lambda p: all_ids.at[me], all_ids.at[me], ids_s, ids_r, d)

    def row_copy(d):
        return to_ex(lambda p: packed.at[p], arrived.at[me], row_s, row_r, d)

    def cot_copy(d):
        return to_ex(lambda p: send_cot.at[p], cot_all.at[grp, me], cot_s, cot_r, d)

    def nrm_copy(d, j):
        return to_ex(
            lambda p: send_rows.at[p, j], rows_all.at[grp, j, me], nrm_s.at[j], nrm_r.at[j], d
        )

    def ret_copy(d, j):
        return to_ex(lambda p: expert_out.at[j, p], returned.at[me, j], ret_s.at[j], ret_r.at[j], d)

    def across(held, send, recv, d):
        peer = lax.rem(chip + d, chips) * 2 + core
        return pltpu.make_async_remote_copy(
            src_ref=held(grp), dst_ref=held(grp), send_sem=send.at[d], recv_sem=recv.at[d],
            device_id={"grp": peer}, device_id_type=MESH,
        )

    def to_mate(held, send, recv, d):
        source = lax.rem(chip - d + chips, chips) * 2 + core
        return pltpu.make_async_remote_copy(
            src_ref=held(source), dst_ref=held(source), send_sem=send.at[d], recv_sem=recv.at[d],
            device_id={"grp": mate}, device_id_type=MESH,
        )

    def cot_across(d):
        return across(lambda b: cot_all.at[b], cx_s, cx_r, d)

    def cot_mate(d):
        return to_mate(lambda b: cot_all.at[b], cm_s, cm_r, d)

    def rows_across(d, j):
        return across(lambda b: rows_all.at[b, j], rx_s.at[j], rx_r.at[j], d)

    def rows_mate(d, j):
        return to_mate(lambda b: rows_all.at[b, j], rm_s.at[j], rm_r.at[j], d)

    ids_row = jnp.concatenate([ids_here[s : s + 1, :] for s in range(seqs)], axis=1)
    all_ids[me] = ids_row
    for d in range(1, n):
        ids_copy(d).start()

    before = (iota((tok, tok), 0) < iota((tok, tok), 1)).astype(BF)
    e0, e1 = e_row[0:1, :], e_row[1:2, :]
    e_iota = iota((experts, tok), 0)
    hot0, hot1 = e_iota == e0, e_iota == e1
    hot = jnp.where(hot0, 1.0, jnp.where(hot1, 1.0, 0.0)).astype(BF)
    earlier = dot(hot, before)
    slot0 = e0 * CAP + jnp.sum(jnp.where(hot0, earlier, 0.0), axis=0, keepdims=True).astype(jnp.int32)
    slot1 = e1 * CAP + jnp.sum(jnp.where(hot1, earlier, 0.0), axis=0, keepdims=True).astype(jnp.int32)
    g0, g1 = g_row[0:1, :], g_row[1:2, :]
    listed = [e0.astype(F32), e1.astype(F32), g0, g1, ids_row.astype(F32), jnp.zeros((3, tok), F32)]
    columns_of = jnp.concatenate(listed, axis=0).T
    for p in range(n):
        s_iota = iota((block, tok), 0) + p * block
        m0, m1 = s_iota == slot0, s_iota == slot1
        weight = jnp.sum(jnp.where(m0, g0, jnp.where(m1, g1, 0.0)), axis=1, keepdims=True)
        chosen[p] = jnp.where(m0, 1.0, jnp.where(m1, 1.0, 0.0)).astype(BF)
        mine_cot = weight * dot(chosen[p], d_out[...])
        send_cot[p] = mine_cot.astype(BF).reshape(exp_here, CAP, width)
    for d in range(1, n):
        cot_copy(d).start()
    cot_all[grp, me] = send_cot[me]

    for d in range(1, n):
        ids_copy(d).wait_recv()
    ids = jnp.concatenate([all_ids[r] for r in range(n)], axis=0)
    here = ids - me * rows_here
    mine = (here >= 0) & (here < rows_here)
    order = dot(jnp.where(mine, 1.0, 0.0).astype(BF), before)
    keys = jnp.where(mine, order.astype(jnp.int32), -1)
    for r in range(n):
        key[r] = keys[r : r + 1, :]
        local[r] = jnp.where(mine, here, 0)[r : r + 1, :].astype(F32)

    def pick(r):
        hit = iota((row_cap, tok), 0) == key[r]
        return jnp.sum(jnp.where(hit, local[r], 0.0), axis=1, keepdims=True).astype(jnp.int32)

    loads[0].wait()

    @pl.loop(0, n // 2)
    def _(i):
        first = lax.rem(me + 1 + 2 * i, n)
        second = lax.rem(me + 2 + 2 * i, n)
        index = jnp.concatenate([pick(first), pick(second)], axis=0)
        onehot = jnp.where(iota((2 * row_cap, rows_here), 1) == index, 1.0, 0.0).astype(BF)
        got = dot(onehot, table[...]).astype(BF)
        packed[first] = got[:row_cap]
        packed[second] = got[row_cap:]
        row_copy(2 * i + 1).start()

        @pl.when(i < n // 2 - 1)
        def _():
            row_copy(2 * i + 2).start()

    arrived[me] = packed[me]

    ids_c = columns_of[:, 4:5].astype(jnp.int32)
    h_iota = iota((tok, n), 1)
    base = h_iota * rows_here
    hot_h = jnp.where((ids_c >= base) & (ids_c < base + rows_here), 1.0, 0.0)
    after = (iota((tok, tok), 0) > iota((tok, tok), 1)).astype(BF)
    ahead = dot(after, hot_h.astype(BF)) + (h_iota * row_cap).astype(F32)
    place = jnp.sum(ahead * hot_h, axis=1, keepdims=True).astype(jnp.int32)
    find = jnp.where(iota((tok, n * row_cap), 1) == place, 1.0, 0.0).astype(BF)
    t_iota = iota((tok, 1), 0)
    length = tok // seqs
    valid = jnp.zeros((tok, 1), F32)
    for s in range(seqs):
        inside = (t_iota >= s * length) & (t_iota < s * length + lens[s])
        valid = jnp.where(inside, 1.0, valid)
    col = columns_of[:, 0:2].astype(jnp.int32)
    c_iota = iota((tok, experts), 1)
    hots = [c_iota == col[:, k : k + 1] for k in range(TOP)]
    spans = experts * CAP // width
    hot_c = jnp.where(hots[0], 1.0, jnp.where(hots[1], 1.0, 0.0)).astype(BF)
    earlier_c = dot(after, hot_c)
    for k in range(TOP):
        rank = jnp.sum(jnp.where(hots[k], earlier_c, 0.0), axis=1, keepdims=True)
        slot = col[:, k : k + 1] * CAP + rank.astype(jnp.int32)
        for i in range(spans):
            hit = iota((tok, width), 1) + i * width == slot
            table[pl.ds((k * spans + i) * tok, tok)] = jnp.where(hit, 1.0, 0.0).astype(BF)

    for d in range(1, n):
        cot_copy(d).wait_recv()
    for d in range(1, chips):
        cot_across(d).start()
    cot_mate(0).start()

    for d in range(1, n):
        row_copy(d).wait_recv()
    emb = dot(find, arrived[...].reshape(n * row_cap, width))
    emb = jnp.where(valid > 0.5, emb, 0.0)
    out[...] = emb.astype(BF)
    mean_square = jnp.mean(emb * emb, axis=1, keepdims=True)
    normed = (emb * lax.rsqrt(mean_square + EPSILON) * gain[...]).astype(BF)
    for p in range(n):
        send_rows[p] = dot(chosen[p], normed).astype(BF).reshape(exp_here, CAP, width)

    @pl.loop(0, exp_here)
    def _(j):
        for d in range(1, n):
            nrm_copy(d, j).start()
        rows_all[grp, j, me] = send_rows[me, j]

    for d in range(1, chips):
        cot_across(d).wait_recv()
        cot_mate(d).start()
    for load in loads[1:]:
        load.wait()

    @pl.loop(0, exp_here)
    def _(j):
        for d in range(1, n):
            nrm_copy(d, j).wait_recv()
        for d in range(1, chips):
            rows_across(d, j).start()
        rows_mate(0, j).start()
        x = rows_all[grp, j].reshape(n * CAP, width)
        gate = dot(x, w_gate[j])
        up = dot(x, w_up[j])
        active = (gate * sigmoid_of(gate) * up).astype(BF)
        result = dot(active, w_down[j], ((1,), (1,))).astype(BF)
        expert_out[j] = result.reshape(n, CAP, width)
        for d in range(1, n):
            ret_copy(d, j).start()
        returned[me, j] = expert_out[j, me]

    for d in range(chips):
        cot_mate(d).wait_recv()

    def pass_on(j):
        for d in range(1, chips):
            rows_across(d, j).wait_recv()
            rows_mate(d, j).start()

    def write(j, k):
        target = (o_gate, o_up, o_down)[k]
        return pltpu.make_async_copy(stage.at[j % 2, k], target.at[j], stage_s.at[j % 2, k])

    pass_on(0)
    columns = pl.ds(pl.multiple_of(grp * part, part), part)

    @pl.loop(0, exp_here)
    def _(j):
        @pl.when(j < exp_here - 1)
        def _():
            pass_on(j + 1)

        for d in range(chips):
            rows_mate(d, j).wait_recv()

        @pl.when(j >= 2)
        def _():
            for k in range(3):
                write(j - 2, k).wait()

        few = max(1, min(groups, 256 // (n * n)))
        for b in range(0, groups, few):
            some = pl.ds(b, min(few, groups - b))
            x = rows_all[some, j].reshape(-1, width)
            c = cot_all[some, :, j].reshape(-1, width)
            gate = dot(x, w_gate[j, :, columns])
            up = dot(x, w_up[j, :, columns])
            d_active = dot(c, w_down[j, :, columns])
            sigmoid = sigmoid_of(gate)
            silu = gate * sigmoid
            active = (silu * up).astype(BF)
            d_gate = (d_active * up * sigmoid * (1.0 + gate * (1.0 - sigmoid))).astype(BF)
            d_up = (d_active * silu).astype(BF)
            for k, (left, right) in enumerate([(x, d_gate), (x, d_up), (c, active)]):
                term = dot(left, right, ((0,), (0,)))
                stage[j % 2, k] = term if b == 0 else stage[j % 2, k] + term
        for k in range(3):
            write(j, k).start()

    @pl.loop(0, exp_here)
    def _(j):
        for d in range(1, n):
            ret_copy(d, j).wait_recv()

    back = returned[...].reshape(experts * CAP, width)
    mixed = jnp.zeros((tok, width), F32)
    for k in range(TOP):
        picked = jnp.zeros((tok, width), F32)
        for i in range(spans):
            pick_part = table[pl.ds((k * spans + i) * tok, tok)]
            picked = picked + dot(pick_part, back[i * width : (i + 1) * width])
        mixed = mixed + columns_of[:, 2 + k : 3 + k] * picked
    out[...] = (out[...].astype(F32) + mixed).astype(BF)

    for j in range(max(0, exp_here - 2), exp_here):
        for k in range(3):
            write(j, k).wait()
    for d in range(1, n):
        for copy in (ids_copy, row_copy, cot_copy):
            copy(d).wait_send()
    for d in range(1, chips):
        cot_across(d).wait_send()
    for d in range(chips):
        cot_mate(d).wait_send()

    @pl.loop(0, exp_here)
    def _(j):
        for d in range(1, n):
            nrm_copy(d, j).wait_send()
            ret_copy(d, j).wait_send()
        for d in range(1, chips):
            rows_across(d, j).wait_send()
        for d in range(chips):
            rows_mate(d, j).wait_send()


def on_device(
    item_ids, lengths, expert_ids, gate_weights, table, norm_gain, w_gate, w_up, w_down, d_out
):
    n = lax.axis_size("ex")
    groups = lax.axis_size("grp")
    seqs, length = item_ids.shape
    tok = seqs * length
    width = table.shape[1]
    exp_here, _, hidden = w_gate.shape
    part = hidden // groups
    experts = exp_here * n
    row_cap = tok // 4
    block = exp_here * CAP
    chips = groups // 2
    vmem = pl.BlockSpec(memory_space=pltpu.VMEM)
    hbm = pl.BlockSpec(memory_space=pl.ANY)
    dma = pltpu.SemaphoreType.DMA
    grad = jax.ShapeDtypeStruct((exp_here, width, part), F32)
    return pl.pallas_call(
        functools.partial(layer_kernel, n, groups, seqs, experts, row_cap),
        out_shape=(jax.ShapeDtypeStruct((tok, width), BF), grad, grad, grad),
        in_specs=[vmem, pl.BlockSpec(memory_space=pltpu.SMEM)] + [vmem] * 4 + [hbm] * 4,
        out_specs=(vmem, hbm, hbm, hbm),
        scratch_shapes=[
            pltpu.VMEM((n, 1, tok), jnp.int32),
            pltpu.VMEM((n, 1, tok), jnp.int32),
            pltpu.VMEM((n, 1, tok), F32),
            pltpu.VMEM((n, row_cap, width), BF),
            pltpu.VMEM((n, row_cap, width), BF),
            pltpu.VMEM((n, block, tok), BF),
            pltpu.VMEM((n, exp_here, CAP, width), BF),
            pltpu.VMEM((n, exp_here, CAP, width), BF),
            pltpu.VMEM((groups, exp_here, n, CAP, width), BF),
            pltpu.VMEM((groups, n, exp_here, CAP, width), BF),
            pltpu.VMEM((exp_here, n, CAP, width), BF),
            pltpu.VMEM((n, exp_here, CAP, width), BF),
            pltpu.VMEM(table.shape, BF),
            pltpu.VMEM(w_gate.shape, BF),
            pltpu.VMEM(w_up.shape, BF),
            pltpu.VMEM(w_down.shape, BF),
            pltpu.VMEM((2, 3, width, part), F32),
        ]
        + [dma((n,))] * 6
        + [dma((exp_here, n))] * 4
        + [dma((chips,))] * 4
        + [dma((exp_here, chips))] * 4
        + [dma((4,)), dma((2, 3))],
        compiler_params=pltpu.CompilerParams(
            collective_id=0, has_side_effects=True, vmem_limit_bytes=VMEM_BYTES
        ),
    )(
        item_ids,
        lengths,
        expert_ids.T,
        gate_weights.T,
        norm_gain.reshape(1, width),
        d_out,
        table,
        w_gate,
        w_up,
        w_down,
    )


def solution(mesh):
    placed = (
        P(("grp", "ex"), None),
        P(("grp", "ex")),
        P(("grp", "ex"), None),
        P(("grp", "ex"), None),
        P("ex", None),
        P(),
        P("ex", None, None),
        P("ex", None, None),
        P("ex", None, None),
        P(("grp", "ex"), None),
    )
    return jax.shard_map(
        on_device,
        mesh=mesh,
        in_specs=placed,
        out_specs=(
            P(("grp", "ex"), None),
            P("ex", None, "grp"),
            P("ex", None, "grp"),
            P("ex", None, "grp"),
        ),
        check_vma=False,
    )
```
